256 devices in a mesh: op: 16 (over x, y), tm: 16 (over z, core).
Axes of the slice: x: 4, y: 4, z: 8, core: 2. Of those that a mesh axis runs over, the one named last changes fastest.
Arguments:
- elementals: bfloat16 [128, 32, 256, 256], P('op', 'tm'), may hold values from -6 to 6
- perambulators: bfloat16 [32, 4, 256, 256], P('tm'), may hold values from -0.375 to 0.375
- src_times: int32 [4], replicated, may hold values from 0 to 31, as said below
- pair_ops: int32 [2048, 2], replicated, may hold values from 0 to 127, as said below
- conj_flags: int32 [2048], replicated, may hold values 0 or 1
Outputs:
- correlator: float32 [2048, 32, 4], P('op', 'tm')
The draws below stay inside these ranges and needn't reach their ends.
Inputs may be any that keep to these rules, and one draw needn't show every extreme that they name: `src_times`: the 4 entries are different timeslices, one of them the last. `pair_ops`: the two operators of a pair have equal numbers modulo 4.
All inputs are finite; a program needn't handle non-finite values.
Results may differ from the reference program's by a relative error of at most 0.0041.
Values may be sent and summed in bfloat16 or wider, within the bound.
No kernel may reach another device: no remote copies, remote signals or barrier semaphores. Data moves between devices by JAX's collectives and lax.ppermute only.
A program may use at most 128 MiB of HBM per device.

```python
import jax
import jax.numpy as jnp
from jax import lax

N_MODES = 256
TSRC = 4
IRREPS = 4
OPS = 128
TIMES = 32
PAIRS = 2048


def draw_src_times(key, part):
    key = jax.random.fold_in(key, 11)
    pick_key, order_key = jax.random.split(key)
    others = jax.random.permutation(pick_key, TIMES - 1)[:TSRC - 1]
    chosen = jnp.concatenate([jnp.array([TIMES - 1], jnp.int32), others.astype(jnp.int32)])
    order = jax.random.permutation(order_key, TSRC)
    return chosen[order].astype(jnp.int32)


def draw_pair_ops(key, part):
    key = jax.random.fold_in(key, 23)
    first_key, second_key = jax.random.split(key)
    positions = jnp.arange(PAIRS)
    left_ops = jax.random.randint(first_key, (PAIRS,), 0, OPS)
    left_ops = jnp.where(positions == 0, OPS - 1, left_ops)
    left_ops = jnp.where(positions == 1, 0, left_ops)
    stride_pick = jax.random.randint(second_key, (PAIRS,), 0, OPS // IRREPS)
    right_ops = left_ops % IRREPS + IRREPS * stride_pick
    right_ops = jnp.where(positions == 1, 0, right_ops)
    return jnp.stack([left_ops, right_ops], 1).astype(jnp.int32)


def touch_ends(drawn, stream_key, smallest, largest):
    extent = drawn.shape
    index_at = [jax.random.randint(jax.random.fold_in(stream_key, axis), (), 0, extent[axis]) for axis in range(len(extent))]
    drawn = drawn.at[tuple(index_at)].set(smallest)
    longest = extent.index(max(extent))
    index_at[longest] = (index_at[longest] + 1) % extent[longest]
    return drawn.at[tuple(index_at)].set(largest)


def block_scale(rng, dims, cuts, low, high):
    gain, own = 1.0, jax.random.fold_in(rng, 6)
    for position, parts in cuts:
        heights = jnp.exp(jax.random.uniform(jax.random.fold_in(own, position), (parts,), jnp.float32, low / len(cuts), high / len(cuts)))
        gain = gain * jnp.repeat(heights, dims[position] // parts).reshape([-1 if axis == position else 1 for axis in range(len(dims))])
    return gain


def scatter_about(stream_key, shape, deviation, bound, cuts=(), dtype=jnp.bfloat16):
    factor_of = block_scale(stream_key, shape, cuts, -0.22, 0.18) if cuts else 1.0
    values = jax.random.normal(stream_key, shape, jnp.float32) * deviation * factor_of
    return jnp.minimum(jnp.maximum(values, -bound), bound).astype(dtype)


def setup_inputs(seed: int = 0) -> dict:
    arg_keys = jax.random.split(jax.random.key(seed), 6)
    return {
        "elementals": scatter_about(arg_keys[0], (OPS, TIMES, N_MODES, N_MODES), 1.0, 6.0, ((0, 16), (1, 16))),
        "perambulators": scatter_about(arg_keys[1], (TIMES, TSRC, N_MODES, N_MODES), N_MODES ** -0.5, 0.375, ((0, 16),)),
        "src_times": draw_src_times(jax.random.fold_in(arg_keys[5], 71), 0),
        "pair_ops": draw_pair_ops(jax.random.fold_in(arg_keys[5], 71), 0),
        "conj_flags": touch_ends((jax.random.randint(arg_keys[4], (PAIRS,), 0, 2) < 1).astype(jnp.int32), jax.random.fold_in(arg_keys[4], 1), 0, 1),
    }


def reference(elementals, perambulators, src_times, pair_ops, conj_flags):
    mode_count = elementals.shape[-1]
    flat_size = mode_count * mode_count
    source = jnp.take(elementals, src_times.astype(jnp.int32), axis=1)
    source_flat = source.reshape(OPS, TSRC, flat_size).astype(jnp.float32)
    propagate = perambulators.astype(jnp.float32)

    def sink_row(element):
        half_product = jnp.einsum('tij,tkjl->tkil', element.astype(jnp.float32), propagate).astype(jnp.bfloat16)
        sandwich = jnp.einsum('tkji,tkjl->tkil', propagate, half_product.astype(jnp.float32)).astype(jnp.bfloat16)
        sandwich = sandwich.reshape(TIMES, TSRC, flat_size).astype(jnp.float32)
        return jnp.einsum('tkx,bkx->tkb', sandwich, source_flat)

    products = lax.map(sink_row, elementals)
    left_ops = pair_ops[:, 0].astype(jnp.int32)
    right_ops = pair_ops[:, 1].astype(jnp.int32)
    forward = products[left_ops, :, :, right_ops]
    backward = products[right_ops, :, :, left_ops]
    mirrored = conj_flags[:, None, None] == 1
    symmetric = jnp.where(mirrored, 0.5 * (forward + backward), forward)
    return symmetric / mode_count
```

```python
import jax
import jax.numpy as jnp
from jax import lax
from jax.experimental import pallas as pl
from jax.experimental.pallas import tpu as pltpu
from jax.sharding import Mesh, PartitionSpec as P

CLASSES = 4
LANES = 128
F32 = jnp.float32
BF16 = jnp.bfloat16


def shift(block, axis, step):
    size = lax.axis_size(axis)
    return lax.ppermute(block, axis, [(i, (i + step) % size) for i in range(size)])


def sandwich_kernel(e_ref, p_ref, pt_ref, w_ref, wide):
    ops, modes = e_ref.shape[0], e_ref.shape[2]
    for a in range(ops):
        half = jnp.dot(e_ref[a, 0], p_ref[0], preferred_element_type=F32).astype(BF16)
        whole = jnp.dot(pt_ref[0], half, preferred_element_type=F32)
        for part in range(modes // LANES):
            wide[part, pl.ds(a, modes, stride=ops), :] = whole[:, part * LANES : (part + 1) * LANES]
    for part in range(modes // LANES):
        w_ref[:, :, part * LANES : (part + 1) * LANES] = wide[part].reshape(modes, ops, LANES).astype(BF16)


def sandwiches(elements, props, props_t):
    ops, times, modes, _ = elements.shape
    return pl.pallas_call(
        sandwich_kernel,
        grid=(times,),
        in_specs=[
            pl.BlockSpec((ops, 1, modes, modes), lambda t: (0, t, 0, 0)),
            pl.BlockSpec((1, modes, modes), lambda t: (t, 0, 0)),
            pl.BlockSpec((1, modes, modes), lambda t: (t, 0, 0)),
        ],
        out_specs=pl.BlockSpec((modes, ops, modes), lambda t: (0, t, 0)),
        out_shape=jax.ShapeDtypeStruct((modes, times * ops, modes), BF16),
        scratch_shapes=[pltpu.VMEM((modes // LANES, modes * ops, LANES), F32)],
        compiler_params=pltpu.CompilerParams(vmem_limit_bytes=32 * 2**20),
        cost_estimate=pl.CostEstimate(
            flops=4 * ops * times * modes**3, bytes_accessed=4 * ops * times * modes**2, transcendentals=0
        ),
    )(elements, props, props_t)


def product_kernel(at_ref, wa_ref, wb_ref, s_ref, o_ref):
    rows = s_ref.shape[0]
    sources = jnp.concatenate([s_ref[r] for r in range(rows)], 1)
    for half, w_ref in enumerate((wa_ref, wb_ref)):
        left = jnp.concatenate([w_ref[r] for r in range(rows)], 1)
        o_ref[half] = lax.dot_general(left, sources, (((1,), (1,)), ((), ())), preferred_element_type=F32)


def block_products(at, near, far, sources):
    rows, count, modes = sources.shape
    left = near.shape[1]
    return pl.pallas_call(
        product_kernel,
        grid_spec=pltpu.PrefetchScalarGridSpec(
            num_scalar_prefetch=1,
            grid=(1,),
            in_specs=[
                pl.BlockSpec((rows, left, modes), lambda i, at: (at[0], 0, 0)),
                pl.BlockSpec((rows, left, modes), lambda i, at: (at[0], 0, 0)),
                pl.BlockSpec((rows, count, modes), lambda i, at: (0, 0, 0)),
            ],
            out_specs=pl.BlockSpec((2, left, count), lambda i, at: (0, 0, 0)),
        ),
        out_shape=jax.ShapeDtypeStruct((2, left, count), F32),
        compiler_params=pltpu.CompilerParams(vmem_limit_bytes=32 * 2**20),
        cost_estimate=pl.CostEstimate(
            flops=4 * rows * left * count * modes,
            bytes_accessed=2 * rows * modes * (2 * left + count),
            transcendentals=0,
        ),
    )(at.reshape(1).astype(jnp.int32), near, far, sources)


def scatter_z(chunk):
    z, size = lax.axis_index("z"), lax.axis_size("z")
    reach = size // 2
    up = down = None
    for step in range(reach):
        mine = chunk((z + size - (reach - step)) % size)
        down = shift(mine if down is None else mine + down, "z", -1)
        if step:
            mine = chunk((z + reach - step) % size)
            up = shift(mine if up is None else mine + up, "z", 1)
    return chunk(z) + up + down


def gather_z(block):
    reach = lax.axis_size("z") // 2
    found = [(0, block)]
    up = down = block
    for step in range(1, reach):
        up, down = shift(up, "z", 1), shift(down, "z", -1)
        found += [(-step, up), (step, down)]
    half = block.shape[0] // 2
    last = jnp.concatenate([shift(up[:half], "z", 1), shift(down[half:], "z", -1)], 0)
    return found + [(reach, last)]


def per_device(elementals, perambulators, src_times, pair_ops, conj_flags):
    ops, times, modes, _ = elementals.shape
    sources = perambulators.shape[1]
    z, core = lax.axis_index("z"), lax.axis_index("c")
    planes = lax.axis_size("z")
    chips = lax.axis_size("x") * lax.axis_size("y")
    place = lax.axis_index("x") * lax.axis_size("y") + lax.axis_index("y")
    k_half = place % 2
    my_k = 2 * k_half + core
    xy = ("x", "y")

    spread = jnp.broadcast_to(elementals[:, None], (ops, 2, times, modes, modes)).reshape(chips, times, modes, modes)

    beside = shift(elementals, "c", 1)
    slots = []
    for kh in range(2):
        when = src_times[2 * kh + core]
        inside = when % times
        own = lax.dynamic_index_in_dim(elementals, inside, 1, keepdims=False)
        other = lax.dynamic_index_in_dim(beside, inside, 1, keepdims=False)
        holder = when // times
        held = jnp.where(holder % 2 == core, own, other)
        slots.append(jnp.where(holder // 2 == z, held, jnp.zeros_like(held)))
    slots = jnp.stack(slots)
    rows = modes // planes
    mine = scatter_z(lambda j: lax.dynamic_slice_in_dim(slots, j * rows, rows, 2))

    spread = lax.all_to_all(spread, xy, 0, 0, tiled=True)

    mine = mine.reshape(2, 2, CLASSES, rows, modes).transpose(2, 0, 1, 3, 4)
    mine = jnp.broadcast_to(mine[None], (2,) + mine.shape).reshape(chips, 2, rows, modes)
    mine = lax.all_to_all(mine, xy, 0, 0, tiled=True)
    mine = mine.reshape(2 * chips, rows, modes).transpose(1, 0, 2)

    props_near = lax.dynamic_index_in_dim(perambulators, my_k, 1, keepdims=False)
    props_far = shift(lax.dynamic_index_in_dim(perambulators, 2 * k_half + 1 - core, 1, keepdims=False), "c", 1)
    spread_far = shift(spread, "c", 1)
    near = sandwiches(spread, props_near, jnp.swapaxes(props_near, 1, 2))
    far = sandwiches(spread_far, props_far, jnp.swapaxes(props_far, 1, 2))

    total = None
    for offset, block in gather_z(mine):
        part = block_products((z + planes + offset) % planes, near, far, block)
        total = part if total is None else total + part
    by_core = jnp.where(core == 0, total, total[::-1])
    by_core = by_core.reshape(2, 8, -1)
    out = jnp.broadcast_to(by_core[None], (chips,) + by_core.shape).reshape((2 * chips,) + by_core.shape[1:])
    out = lax.all_to_all(out, ("x", "y", "c"), 0, 0, tiled=True)
    groups = 2 * chips
    table = out.reshape(2, CLASSES, 2, 2, times, chips, groups).transpose(5, 0, 1, 4, 2, 3, 6)
    table = table.reshape(CLASSES * groups, times * sources * groups)

    pairs = pair_ops.shape[0] // chips
    local = lax.dynamic_slice_in_dim(pair_ops, place * pairs, pairs, 0)
    flags = lax.dynamic_slice_in_dim(conj_flags, place * pairs, pairs, 0)
    left, right = local[:, 0], local[:, 1]

    def picked(first, second):
        row = (first[:, None] == jnp.arange(CLASSES * groups)[None]).astype(F32)
        lines = jnp.dot(row, table, precision=lax.Precision.HIGHEST, preferred_element_type=F32)
        lines = lines.reshape(pairs, times * sources, groups)
        column = (second // CLASSES)[:, None, None] == jnp.arange(groups)[None, None]
        return jnp.sum(jnp.where(column, lines, 0.0), 2)

    forward, backward = picked(left, right), picked(right, left)
    symmetric = jnp.where(flags[:, None] == 1, 0.5 * (forward + backward), forward)
    return (symmetric / modes).reshape(pairs, times, sources)


def solution(mesh):
    chips = Mesh(mesh.devices.reshape(4, 4, 8, 2), ("x", "y", "z", "c"))
    op, tm = ("x", "y"), ("z", "c")
    return jax.shard_map(
        per_device,
        mesh=chips,
        in_specs=(P(op, tm, None, None), P(tm, None, None, None), P(), P(), P()),
        out_specs=P(op, tm, None),
        check_vma=False,
    )
```

```python
import jax
import jax.numpy as jnp
from jax import lax
from jax.experimental import pallas as pl
from jax.experimental.pallas import tpu as pltpu
from jax.experimental.layout import Layout, with_layout_constraint
from jax.sharding import Mesh, PartitionSpec as P

CLASSES = 4
LANES = 128
F32 = jnp.float32
BF16 = jnp.bfloat16


def shift(block, axis, step):
    size = lax.axis_size(axis)
    return lax.ppermute(block, axis, [(i, (i + step) % size) for i in range(size)])


def sandwich_kernel(e_ref, p_ref, w_ref, wide):
    ops, modes = e_ref.shape[:2]
    prop = p_ref[...]
    turned = prop.T
    for a in range(ops):
        half = jnp.dot(e_ref[a], prop, preferred_element_type=F32).astype(BF16)
        whole = jnp.dot(turned, half, preferred_element_type=F32)
        for part in range(modes // LANES):
            wide[part, pl.ds(a, modes, stride=ops), :] = whole[:, part * LANES : (part + 1) * LANES]
    for part in range(modes // LANES):
        w_ref[:, :, part * LANES : (part + 1) * LANES] = wide[part].reshape(modes, ops, LANES).astype(BF16)


def sandwiches(elements, prop):
    ops, modes, _ = elements.shape
    return pl.pallas_call(
        sandwich_kernel,
        out_shape=jax.ShapeDtypeStruct((modes, ops, modes), BF16),
        scratch_shapes=[pltpu.VMEM((modes // LANES, modes * ops, LANES), F32)],
        compiler_params=pltpu.CompilerParams(vmem_limit_bytes=16 * 2**20),
        cost_estimate=pl.CostEstimate(
            flops=4 * ops * modes**3, bytes_accessed=4 * ops * modes**2, transcendentals=0
        ),
    )(elements, prop)


def double_kernel(time, e_ref, o_ref, held, get_sem, put_sem):
    get = pltpu.make_async_copy(e_ref.at[:, time], held, get_sem)
    puts = [pltpu.make_async_copy(held, o_ref.at[:, twin], put_sem.at[twin]) for twin in range(2)]
    get.start()
    get.wait()
    for put in puts:
        put.start()
    for put in puts:
        put.wait()


def doubled(elements, time, limit):
    ops, _, modes, _ = elements.shape
    out = pl.pallas_call(
        lambda *refs: double_kernel(time, *refs),
        in_specs=[pl.BlockSpec(memory_space=pl.ANY)],
        out_specs=pl.BlockSpec(memory_space=pl.ANY),
        out_shape=jax.ShapeDtypeStruct((ops, 2, modes, modes), BF16),
        scratch_shapes=[
            pltpu.VMEM((ops, modes, modes), BF16),
            pltpu.SemaphoreType.DMA(()),
            pltpu.SemaphoreType.DMA((2,)),
        ],
        compiler_params=pltpu.CompilerParams(vmem_limit_bytes=limit * 2**20),
        cost_estimate=pl.CostEstimate(flops=2**32, bytes_accessed=6 * ops * modes**2, transcendentals=0),
    )(elements)
    return out.reshape(2 * ops, modes, modes)


def slot_kernel(when_ref, own_ref, other_ref, o_ref, zeros, sem):
    z, core = lax.axis_index("z"), lax.axis_index("c")
    times, count = own_ref.shape[1], o_ref.shape[0]
    zeros[...] = jnp.zeros_like(zeros)
    for slot in range(count):
        when = when_ref[2 * slot + core]
        holder, inside = when // times, when % times
        here = holder // 2 == z
        mine = here & (holder % 2 == core)

        def fetch(source, slot=slot):
            pltpu.make_async_copy(source, o_ref.at[slot], sem.at[slot]).start()

        pl.when(mine)(lambda inside=inside, fetch=fetch: fetch(own_ref.at[:, inside]))
        pl.when(here & ~mine)(lambda inside=inside, fetch=fetch: fetch(other_ref.at[:, inside]))
        pl.when(~here)(lambda fetch=fetch: fetch(zeros))
    for slot in range(count):
        pltpu.make_async_copy(zeros, o_ref.at[slot], sem.at[slot]).wait()


def slots_of(src_times, own, other):
    ops, _, modes, _ = own.shape
    count = src_times.shape[0] // 2
    return pl.pallas_call(
        slot_kernel,
        in_specs=[pl.BlockSpec(memory_space=pltpu.SMEM)] + [pl.BlockSpec(memory_space=pl.ANY)] * 2,
        out_specs=pl.BlockSpec(memory_space=pltpu.VMEM),
        out_shape=jax.ShapeDtypeStruct((count, ops, modes, modes), BF16),
        scratch_shapes=[pltpu.VMEM((ops, modes, modes), BF16), pltpu.SemaphoreType.DMA((count,))],
        compiler_params=pltpu.CompilerParams(vmem_limit_bytes=8 * 2**20),
    )(src_times, own, other)


def product_kernel(tasks, at_ref, *refs):
    lefts, blocks, outs = refs[: 2 * len(tasks)], refs[2 * len(tasks) : -len(tasks)], refs[-len(tasks) :]
    rows = blocks[0].shape[0]
    for task, numbers in enumerate(tasks):
        total = None
        for number in numbers:
            sources = jnp.concatenate([blocks[number][r] for r in range(rows)], 1)
            base = at_ref[number] * rows
            pair = lefts[2 * task : 2 * task + 2]
            left = jnp.concatenate([jnp.concatenate([w[base + r] for w in pair], 0) for r in range(rows)], 1)
            part = lax.dot_general(left, sources, (((1,), (1,)), ((), ())), preferred_element_type=F32)
            total = part if total is None else total + part
        outs[task][...] = total


def block_products(tasks, found):
    rows, count, modes = found[0][1].shape
    left = tasks[0][0][0].shape[1]
    work = sum(len(numbers) for _, numbers in tasks)
    return pl.pallas_call(
        lambda *refs: product_kernel([numbers for _, numbers in tasks], *refs),
        in_specs=[pl.BlockSpec(memory_space=pltpu.SMEM)]
        + [pl.BlockSpec(memory_space=pltpu.VMEM)] * (2 * len(tasks) + len(found)),
        out_shape=[jax.ShapeDtypeStruct((2 * left, count), F32)] * len(tasks),
        compiler_params=pltpu.CompilerParams(vmem_limit_bytes=8 * 2**20),
        cost_estimate=pl.CostEstimate(
            flops=4 * work * rows * left * count * modes,
            bytes_accessed=2 * work * rows * modes * (2 * left + count),
            transcendentals=0,
        ),
    )(
        jnp.stack([at for at, _ in found]).astype(jnp.int32),
        *[w for pair, _ in tasks for w in pair],
        *[block for _, block in found],
    )


def per_device(elementals, perambulators, src_times, pair_ops, conj_flags):
    ops, times, modes, _ = elementals.shape
    sources = perambulators.shape[1]
    z, core = lax.axis_index("z"), lax.axis_index("c")
    planes = lax.axis_size("z")
    chips = lax.axis_size("x") * lax.axis_size("y")
    place = lax.axis_index("x") * lax.axis_size("y") + lax.axis_index("y")
    k_half = place % 2
    my_k = 2 * k_half + core
    xy = ("x", "y")

    tie = lambda *values: lax.optimization_barrier(values)
    props_near = lax.dynamic_index_in_dim(perambulators, my_k, 1, keepdims=False)
    props_far = lax.dynamic_index_in_dim(perambulators, 2 * k_half + 1 - core, 1, keepdims=False)

    double = doubled(elementals, 0, 60)

    beside = shift(elementals, "c", 1)
    beside, double = tie(beside, double)
    slots = slots_of(src_times, elementals, beside)

    rows, reach = modes // planes, planes // 2
    chunk = lambda j: lax.dynamic_slice_in_dim(slots, j % planes * rows, rows, 2)
    down = shift(chunk(z + planes - reach), "z", -1)
    first = lax.all_to_all(double, xy, 0, 0, tiled=True)
    up = None
    for step in range(1, reach):
        send_down = chunk(z + planes - reach + step) + down
        send_up = chunk(z + reach - step)
        if up is not None:
            send_up = send_up + up
        send_down, send_up = tie(send_down, send_up)
        down, up = shift(send_down, "z", -1), shift(send_up, "z", 1)
        down, up = tie(down, up)
    mine = chunk(z) + up + down
    props_far = shift(props_far, "c", 1)
    first, mine, props_near, props_far = tie(first, mine, props_near, props_far)

    mine = mine.reshape(2, 2, CLASSES, rows, modes).transpose(2, 0, 1, 3, 4)
    mine = jnp.broadcast_to(mine[None], (2,) + mine.shape).reshape(chips, 2 * rows, modes)
    elements, mine = tie(elementals, mine)
    second = lax.all_to_all(doubled(elements, 1, 8), xy, 0, 0, tiled=True)
    mine = lax.all_to_all(mine, xy, 0, 0, tiled=True)
    mine = mine.reshape(2 * chips, rows, modes).transpose(1, 0, 2)

    first_far = shift(first, "c", 1)
    number = lambda offset: (z + planes + offset) % planes
    found = [(number(0), mine)]
    up, down = shift(mine, "z", 1), shift(mine, "z", -1)
    w_near = sandwiches(first, props_near[0])
    up, down, w_near, first_far = tie(up, down, w_near, first_far)
    found += [(number(-1), up), (number(1), down)]
    up, down = shift(up, "z", 1), shift(down, "z", -1)
    w_far = sandwiches(first_far, props_far[0])
    up, down, w_far = tie(up, down, w_far)
    found += [(number(-2), up), (number(2), down)]
    w_first = w_near, w_far
    up, down = shift(up, "z", 1), shift(down, "z", -1)
    (early,) = block_products([(w_first, range(5))], found)
    second, up, down, early = tie(second, up, down, early)
    found += [(number(-3), up), (number(3), down)]
    last = shift(up, "z", 1)
    second_far = shift(second, "c", 1)
    w_second = sandwiches(second, props_near[1]), sandwiches(second_far, props_far[1])
    middle, total = block_products([(w_first, range(5, 7)), (w_second, range(7))], found)
    last, middle = tie(last, middle)
    late = block_products([(w_first, [0]), (w_second, [0])], [(number(reach), last)])
    early, total = early + middle + late[0], total + late[1]
    total = jnp.stack([early.reshape(2, -1), total.reshape(2, -1)], 1)
    by_core = jnp.where(core == 0, total, total[::-1])
    by_core = by_core.reshape(2, 8, -1)
    out = jnp.broadcast_to(by_core[None], (chips,) + by_core.shape).reshape((2 * chips,) + by_core.shape[1:])
    out = lax.all_to_all(out, ("x", "y", "c"), 0, 0, tiled=True)
    groups = 2 * chips
    table = out.reshape(2, CLASSES, 2, 2, times, chips, groups).transpose(5, 0, 1, 4, 2, 3, 6)
    table = table.reshape(CLASSES * groups, times * sources * groups)

    pairs = pair_ops.shape[0] // chips
    local = lax.dynamic_slice_in_dim(pair_ops, place * pairs, pairs, 0)
    flags = lax.dynamic_slice_in_dim(conj_flags, place * pairs, pairs, 0)
    left, right = local[:, 0], local[:, 1]

    def picked(first, second):
        row = (first[:, None] == jnp.arange(CLASSES * groups)[None]).astype(F32)
        lines = jnp.dot(row, table, precision=lax.Precision.HIGHEST, preferred_element_type=F32)
        lines = lines.reshape(pairs, times * sources, groups)
        column = (second // CLASSES)[:, None, None] == jnp.arange(groups)[None, None]
        return jnp.sum(jnp.where(column, lines, 0.0), 2)

    forward, backward = picked(left, right), picked(right, left)
    symmetric = jnp.where(flags[:, None] == 1, 0.5 * (forward + backward), forward)
    return (symmetric / modes).reshape(pairs, times, sources)


def solution(mesh):
    chips = Mesh(mesh.devices.reshape(4, 4, 8, 2), ("x", "y", "z", "c"))
    op, tm = ("x", "y"), ("z", "c")
    return jax.shard_map(
        per_device,
        mesh=chips,
        in_specs=(P(op, tm, None, None), P(tm, None, None, None), P(), P(), P()),
        out_specs=P(op, tm, None),
        check_vma=False,
    )
```

```python
import jax
import jax.numpy as jnp
from jax import lax
from jax.experimental import pallas as pl
from jax.experimental.pallas import tpu as pltpu
from jax.experimental.layout import Layout, with_layout_constraint
from jax.sharding import Mesh, PartitionSpec as P

CLASSES = 4
LANES = 128
F32 = jnp.float32
BF16 = jnp.bfloat16


def shift(block, axis, step):
    size = lax.axis_size(axis)
    return lax.ppermute(block, axis, [(i, (i + step) % size) for i in range(size)])


def sandwich_kernel(e_ref, p_ref, w_ref, wide):
    ops, modes = e_ref.shape[:2]
    prop = p_ref[...]
    turned = prop.T
    for a in range(ops):
        half = jnp.dot(e_ref[a], prop, preferred_element_type=F32).astype(BF16)
        whole = jnp.dot(turned, half, preferred_element_type=F32)
        for part in range(modes // LANES):
            wide[part, pl.ds(a, modes, stride=ops), :] = whole[:, part * LANES : (part + 1) * LANES]
    for part in range(modes // LANES):
        w_ref[:, :, part * LANES : (part + 1) * LANES] = wide[part].reshape(modes, ops, LANES).astype(BF16)


def sandwiches(elements, prop, flops=None):
    ops, modes, _ = elements.shape
    return pl.pallas_call(
        sandwich_kernel,
        out_shape=jax.ShapeDtypeStruct((modes, ops, modes), BF16),
        scratch_shapes=[pltpu.VMEM((modes // LANES, modes * ops, LANES), F32)],
        compiler_params=pltpu.CompilerParams(vmem_limit_bytes=16 * 2**20),
        cost_estimate=pl.CostEstimate(
            flops=4 * ops * modes**3 if flops is None else flops,
            bytes_accessed=4 * ops * modes**2 if flops is None else flops,
            transcendentals=0,
        ),
    )(elements, prop)


def double_kernel(time, e_ref, o_ref, sem):
    puts = [pltpu.make_async_copy(e_ref.at[:, time], o_ref.at[:, twin], sem.at[twin]) for twin in range(2)]
    for put in puts:
        put.start()
    for put in puts:
        put.wait()


def doubled(elements, time):
    ops, _, modes, _ = elements.shape
    out = pl.pallas_call(
        lambda *refs: double_kernel(time, *refs),
        in_specs=[pl.BlockSpec(memory_space=pltpu.VMEM)],
        out_specs=pl.BlockSpec(memory_space=pl.ANY),
        out_shape=jax.ShapeDtypeStruct((ops, 2, modes, modes), BF16),
        scratch_shapes=[pltpu.SemaphoreType.DMA((2,))],
        compiler_params=pltpu.CompilerParams(vmem_limit_bytes=8 * 2**20),
        cost_estimate=pl.CostEstimate(flops=2**32, bytes_accessed=6 * ops * modes**2, transcendentals=0),
    )(elements)
    return out.reshape(2 * ops, modes, modes)


def slot_kernel(when_ref, own_ref, other_ref, o_ref, sem):
    z, core = lax.axis_index("z"), lax.axis_index("c")
    times, count = own_ref.shape[1], o_ref.shape[0]
    for slot in range(count):
        when = when_ref[2 * slot + core]
        holder, inside = when // times, when % times
        here = holder // 2 == z
        mine = here & (holder % 2 == core)

        def fetch(source, slot=slot):
            copy = pltpu.make_async_copy(source, o_ref.at[slot], sem.at[slot])
            copy.start()
            copy.wait()

        def clear(slot=slot):
            o_ref[slot] = jnp.zeros_like(o_ref[slot])

        pl.when(mine)(lambda inside=inside, fetch=fetch: fetch(own_ref.at[:, inside]))
        pl.when(here & ~mine)(lambda inside=inside, fetch=fetch: fetch(other_ref.at[:, inside]))
        pl.when(~here)(clear)


def slots_of(src_times, own, other):
    ops, _, modes, _ = own.shape
    count = src_times.shape[0] // 2
    return pl.pallas_call(
        slot_kernel,
        in_specs=[pl.BlockSpec(memory_space=pltpu.SMEM)] + [pl.BlockSpec(memory_space=pltpu.VMEM)] * 2,
        out_specs=pl.BlockSpec(memory_space=pltpu.VMEM),
        out_shape=jax.ShapeDtypeStruct((count, ops, modes, modes), BF16),
        scratch_shapes=[pltpu.SemaphoreType.DMA((count,))],
        compiler_params=pltpu.CompilerParams(vmem_limit_bytes=8 * 2**20),
    )(src_times, own, other)


def product_kernel(tasks, at_ref, *refs):
    lefts, blocks, outs = refs[: 2 * len(tasks)], refs[2 * len(tasks) : -len(tasks)], refs[-len(tasks) :]
    rows = blocks[0].shape[0]
    for task, numbers in enumerate(tasks):
        total = None
        for number in numbers:
            sources = jnp.concatenate([blocks[number][r] for r in range(rows)], 1)
            base = at_ref[number] * rows
            pair = lefts[2 * task : 2 * task + 2]
            left = jnp.concatenate([jnp.concatenate([w[base + r] for w in pair], 0) for r in range(rows)], 1)
            part = lax.dot_general(left, sources, (((1,), (1,)), ((), ())), preferred_element_type=F32)
            total = part if total is None else total + part
        outs[task][...] = total


def block_products(tasks, found):
    rows, count, modes = found[0][1].shape
    left = tasks[0][0][0].shape[1]
    work = sum(len(numbers) for _, numbers in tasks)
    return pl.pallas_call(
        lambda *refs: product_kernel([numbers for _, numbers in tasks], *refs),
        in_specs=[pl.BlockSpec(memory_space=pltpu.SMEM)]
        + [pl.BlockSpec(memory_space=pltpu.VMEM)] * (2 * len(tasks) + len(found)),
        out_shape=[jax.ShapeDtypeStruct((2 * left, count), F32)] * len(tasks),
        compiler_params=pltpu.CompilerParams(vmem_limit_bytes=8 * 2**20),
        cost_estimate=pl.CostEstimate(
            flops=4 * work * rows * left * count * modes,
            bytes_accessed=2 * work * rows * modes * (2 * left + count),
            transcendentals=0,
        ),
    )(
        jnp.stack([at for at, _ in found]).astype(jnp.int32),
        *[w for pair, _ in tasks for w in pair],
        *[block for _, block in found],
    )


def per_device(elementals, perambulators, src_times, pair_ops, conj_flags):
    ops, times, modes, _ = elementals.shape
    sources = perambulators.shape[1]
    z, core = lax.axis_index("z"), lax.axis_index("c")
    planes = lax.axis_size("z")
    chips = lax.axis_size("x") * lax.axis_size("y")
    place = lax.axis_index("x") * lax.axis_size("y") + lax.axis_index("y")
    k_half = place % 2
    my_k = 2 * k_half + core
    xy = ("x", "y")

    tie = lambda *values: lax.optimization_barrier(values)
    props_near = lax.dynamic_index_in_dim(perambulators, my_k, 1, keepdims=False)
    props_far = lax.dynamic_index_in_dim(perambulators, 2 * k_half + 1 - core, 1, keepdims=False)

    double = doubled(elementals, 0)

    beside = shift(elementals, "c", 1)
    beside, double = tie(beside, double)
    slots = slots_of(src_times, elementals, beside)

    rows, reach = modes // planes, planes // 2
    chunk = lambda j: lax.dynamic_slice_in_dim(slots, j % planes * rows, rows, 2)
    down = shift(chunk(z + planes - reach), "z", -1)
    first = lax.all_to_all(double, xy, 0, 0, tiled=True)
    up = None
    for step in range(1, reach):
        send_down = chunk(z + planes - reach + step) + down
        send_up = chunk(z + reach - step)
        if up is not None:
            send_up = send_up + up
        send_down, send_up = tie(send_down, send_up)
        down, up = shift(send_down, "z", -1), shift(send_up, "z", 1)
        if step == 2:
            double = doubled(elementals, 1)
            down, up, double = tie(down, up, double)
        else:
            down, up = tie(down, up)
    mine = chunk(z) + up + down
    props_far = shift(props_far, "c", 1)
    first, mine, props_near, props_far = tie(first, mine, props_near, props_far)

    mine = mine.reshape(2, 2, CLASSES, rows, modes).transpose(2, 0, 1, 3, 4)
    mine = jnp.broadcast_to(mine[None], (2,) + mine.shape).reshape(chips, 2 * rows, modes)
    mine = lax.all_to_all(mine, xy, 0, 0, tiled=True)
    mine = mine.reshape(2 * chips, rows, modes).transpose(1, 0, 2)
    double, mine = tie(double, mine)
    second = lax.all_to_all(double, xy, 0, 0, tiled=True)

    first_far = shift(first, "c", 1)
    number = lambda offset: (z + planes + offset) % planes
    found = [(number(0), mine)]
    up, down = shift(mine, "z", 1), shift(mine, "z", -1)
    w_near = sandwiches(first, props_near[0])
    up, down, w_near, first_far = tie(up, down, w_near, first_far)
    found += [(number(-1), up), (number(1), down)]
    up, down = shift(up, "z", 1), shift(down, "z", -1)
    w_far = sandwiches(first_far, props_far[0])
    up, down, w_far = tie(up, down, w_far)
    found += [(number(-2), up), (number(2), down)]
    w_first = w_near, w_far
    up, down = shift(up, "z", 1), shift(down, "z", -1)
    (early,) = block_products([(w_first, range(5))], found)
    up, down, early = tie(up, down, early)
    ring = [(2 * i + c, 2 * ((i + (-1) ** c) % planes) + c) for i in range(planes) for c in range(2)]
    last = lax.ppermute(jnp.where(core == 0, up, down), ("z", "c"), ring)
    second, up, down = tie(second, up, down)
    found += [(number(-3), up), (number(3), down)]
    second_far = shift(second, "c", 1)
    w_second = sandwiches(second, props_near[1], 1), sandwiches(second_far, props_far[1], 1)
    middle, total = block_products([(w_first, range(5, 7)), (w_second, range(7))], found)
    last, middle = tie(last, middle)
    late = block_products([(w_first, [0]), (w_second, [0])], [(number(reach), last)])
    early, total = early + middle + late[0], total + late[1]
    total = jnp.stack([early.reshape(2, -1), total.reshape(2, -1)], 1)
    by_core = jnp.where(core == 0, total, total[::-1])
    by_core = by_core.reshape(2, 8, -1)
    out = jnp.broadcast_to(by_core[None], (chips,) + by_core.shape).reshape((2 * chips,) + by_core.shape[1:])
    out = lax.all_to_all(out, ("x", "y", "c"), 0, 0, tiled=True)
    groups = 2 * chips
    table = out.reshape(2, CLASSES, 2, 2, times, chips, groups).transpose(5, 0, 1, 4, 2, 3, 6)
    table = table.reshape(CLASSES * groups, times * sources * groups)

    pairs = pair_ops.shape[0] // chips
    local = lax.dynamic_slice_in_dim(pair_ops, place * pairs, pairs, 0)
    flags = lax.dynamic_slice_in_dim(conj_flags, place * pairs, pairs, 0)
    left, right = local[:, 0], local[:, 1]

    def picked(first, second):
        row = (first[:, None] == jnp.arange(CLASSES * groups)[None]).astype(F32)
        lines = jnp.dot(row, table, precision=lax.Precision.HIGHEST, preferred_element_type=F32)
        lines = lines.reshape(pairs, times * sources, groups)
        column = (second // CLASSES)[:, None, None] == jnp.arange(groups)[None, None]
        return jnp.sum(jnp.where(column, lines, 0.0), 2)

    forward, backward = picked(left, right), picked(right, left)
    symmetric = jnp.where(flags[:, None] == 1, 0.5 * (forward + backward), forward)
    return (symmetric / modes).reshape(pairs, times, sources)


def solution(mesh):
    chips = Mesh(mesh.devices.reshape(4, 4, 8, 2), ("x", "y", "z", "c"))
    op, tm = ("x", "y"), ("z", "c")
    return jax.shard_map(
        per_device,
        mesh=chips,
        in_specs=(P(op, tm, None, None), P(tm, None, None, None), P(), P(), P()),
        out_specs=P(op, tm, None),
        check_vma=False,
    )
```
